32 devices in a mesh: row: 8 (over z, core), col: 4 (over y, x).
Axes of the slice: x: 2, y: 2, z: 4, core: 2. Of those that a mesh axis runs over, the one named last changes fastest.
Arguments:
- features: bfloat16 [16384, 256], P(('row', 'col')), may hold values from -6 to 6
- blocks: bfloat16 [8, 4, 192, 64, 64], P('row', 'col'), may hold values from -0.3125 to 0.3125
- block_rows: int32 [8, 4, 192], P('row', 'col'), may hold values from 0 to 31
- block_cols: int32 [8, 4, 192], P('row', 'col'), may hold values from 0 to 63
- block_count: int32 [8, 4], P('row', 'col'), may hold values from 1 to 192, as said below
- w_in: bfloat16 [512, 1024], replicated, may hold values from -0.25 to 0.25
- w_mid: bfloat16 [1024, 1024], replicated, may hold values from -0.1875 to 0.1875
- w_out: bfloat16 [1024, 256], replicated, may hold values from -0.1875 to 0.1875
- cotangent: bfloat16 [16384, 256], P(('row', 'col')), may hold values from -6 to 6
Outputs:
- updated: bfloat16 [16384, 256], P(('row', 'col'))
- grad_nodes: bfloat16 [16384, 256], P(('row', 'col'))
- grad_in: float32 [512, 1024], replicated
- grad_mid: float32 [1024, 1024], replicated
- grad_out: float32 [1024, 256], replicated
The draws below stay inside these ranges and needn't reach their ends.
Inputs may be any that keep to these rules, and one draw needn't show every extreme that they name: Only slots below a cell's block_count are used; the busiest cell uses all 192 slots.
All inputs are finite; a program needn't handle non-finite values.
Results may differ from the reference program's by a relative error of at most 0.015.
Values may be sent and summed in bfloat16 or wider, within the bound.
A program may use at most 128 MiB of HBM per device.

```python
import math
import jax
import jax.numpy as jnp
from jax import lax

F = 256
HID = 1024
BLOCK = 64
NODE_DEV = 512
ROW_GROUPS = 8
COL_GROUPS = 4
NODES = 16384
GROUP_ROWS = 2048
GROUP_COLS = 4096
ROW_BLOCKS = 32
COL_BLOCKS = 64
SLOTS = 192


def draw_block_rows(key, part):
    return jax.random.randint(jax.random.fold_in(key, 11), (ROW_GROUPS, COL_GROUPS, SLOTS), 0, ROW_BLOCKS).astype(jnp.int32)


def draw_block_cols(key, part):
    return jax.random.randint(jax.random.fold_in(key, 23), (ROW_GROUPS, COL_GROUPS, SLOTS), 0, COL_BLOCKS).astype(jnp.int32)


def draw_block_count(key, part):
    first = jax.random.randint(jax.random.fold_in(key, 31), (ROW_GROUPS, COL_GROUPS), 1, SLOTS + 1)
    second = jax.random.randint(jax.random.fold_in(key, 37), (ROW_GROUPS, COL_GROUPS), 1, SLOTS + 1)
    base = jnp.maximum(first * second // SLOTS, 1)
    chosen = jax.random.randint(jax.random.fold_in(key, 41), (), 0, ROW_GROUPS * COL_GROUPS)
    cells = jnp.arange(ROW_GROUPS * COL_GROUPS, dtype=jnp.int32).reshape(ROW_GROUPS, COL_GROUPS)
    return jnp.where(cells == chosen, SLOTS, base).astype(jnp.int32)


def shard_levels(key, dims, split, smallest, high):
    gain, own = 1.0, jax.random.fold_in(key, 6)
    for dim, parts in split:
        draws = jnp.exp(jax.random.uniform(jax.random.fold_in(own, dim), (parts,), jnp.float32, smallest / len(split), high / len(split)))
        gain = gain * jnp.repeat(draws, dims[dim] // parts).reshape([-1 if axis == dim else 1 for axis in range(len(dims))])
    return gain


def noise(stream_key, shape, width, bound, split=(), kind=jnp.bfloat16):
    array = width * jax.random.normal(stream_key, shape, jnp.float32)
    if split:
        array = array * shard_levels(stream_key, shape, split, -0.22, 0.18)
    return jnp.clip(array, -bound, bound).astype(kind)


def setup_inputs(seed: int = 0) -> dict:
    splits = jax.random.split(jax.random.key(seed), 10)
    features = noise(splits[0], (NODES, F), 1.0, 6.0, ((0, 32),))
    blocks = noise(splits[1], (ROW_GROUPS, COL_GROUPS, SLOTS, BLOCK, BLOCK), (6 * BLOCK) ** -0.5, 0.3125, ((0, 8), (1, 4)))
    block_rows = draw_block_rows(jax.random.fold_in(splits[9], 71), 0)
    block_cols = draw_block_cols(jax.random.fold_in(splits[9], 71), 0)
    block_count = draw_block_count(jax.random.fold_in(splits[9], 71), 0)
    w_in = noise(splits[5], (2 * F, HID), (2 * F) ** -0.5, 0.25)
    w_mid = noise(splits[6], (HID, HID), HID ** -0.5, 0.1875)
    w_out = noise(splits[7], (HID, F), HID ** -0.5, 0.1875)
    cotangent = noise(splits[8], (NODES, F), 1.0, 6.0, ((0, 32),))
    return dict(features=features, blocks=blocks, block_rows=block_rows, block_cols=block_cols, block_count=block_count, w_in=w_in, w_mid=w_mid, w_out=w_out, cotangent=cotangent)


def silu_grad(value):
    sig = jax.nn.sigmoid(value)
    return sig * (1.0 + value * (1.0 - sig))

def cell_term(cell_blocks, gather_idx, add_idx, count, source, n_dst, transposed):
    picked = source[gather_idx]
    form = 'sba,sbf->saf' if transposed else 'sab,sbf->saf'
    prod = jnp.einsum(form, cell_blocks.astype(jnp.float32), picked.astype(jnp.float32))
    live = (jnp.arange(SLOTS, dtype=jnp.int32) < count).astype(jnp.float32)
    prod = prod * live[:, None, None]
    total = jnp.zeros((n_dst, BLOCK, F), jnp.float32).at[add_idx].add(prod)
    return total.reshape(n_dst * BLOCK, F)

def reference(features, blocks, block_rows, block_cols, block_count, w_in, w_mid, w_out, cotangent):
    grouped = features.reshape(ROW_GROUPS, COL_GROUPS, NODE_DEV, F)

    def row_group(g):

        def add_cell(total, c):
            source = lax.dynamic_index_in_dim(grouped, c, 1, keepdims=False).reshape(COL_BLOCKS, BLOCK, F)
            term = cell_term(blocks[g, c], block_cols[g, c], block_rows[g, c], block_count[g, c], source, ROW_BLOCKS, False)
            return (total + lax.optimization_barrier(term.astype(jnp.bfloat16)).astype(jnp.float32), None)
        total, _ = lax.scan(add_cell, jnp.zeros((GROUP_ROWS, F), jnp.float32), jnp.arange(COL_GROUPS, dtype=jnp.int32))
        return total.astype(jnp.bfloat16)
    aggregated = lax.map(row_group, jnp.arange(ROW_GROUPS, dtype=jnp.int32)).reshape(NODES, F)
    joined = jnp.concatenate([features, aggregated], axis=1)
    pre_one = jnp.dot(joined, w_in, preferred_element_type=jnp.float32)
    act_one = jax.nn.silu(pre_one).astype(jnp.bfloat16)
    pre_two = jnp.dot(act_one, w_mid, preferred_element_type=jnp.float32)
    act_two = jax.nn.silu(pre_two).astype(jnp.bfloat16)
    updated = (features.astype(jnp.float32) + jnp.dot(act_two, w_out, preferred_element_type=jnp.float32)).astype(jnp.bfloat16)
    ratio = 1.0 / math.sqrt(NODES)
    grad_out = jnp.dot(act_two.T, cotangent, preferred_element_type=jnp.float32) * ratio
    grad_pre_two = (jnp.dot(cotangent, w_out.T, preferred_element_type=jnp.float32) * silu_grad(pre_two)).astype(jnp.bfloat16)
    grad_mid = jnp.dot(act_one.T, grad_pre_two, preferred_element_type=jnp.float32) * ratio
    grad_pre_one = (jnp.dot(grad_pre_two, w_mid.T, preferred_element_type=jnp.float32) * silu_grad(pre_one)).astype(jnp.bfloat16)
    grad_in = jnp.dot(joined.T, grad_pre_one, preferred_element_type=jnp.float32) * ratio
    grad_joined = jnp.dot(grad_pre_one, w_in.T, preferred_element_type=jnp.float32)
    direct = cotangent.astype(jnp.float32) + grad_joined[:, :F]
    grad_agg = grad_joined[:, F:].astype(jnp.bfloat16)
    row_grads = grad_agg.reshape(ROW_GROUPS, ROW_BLOCKS, BLOCK, F)

    def col_group(c):

        def add_cell(total, g):
            source = lax.dynamic_index_in_dim(row_grads, g, 0, keepdims=False)
            term = cell_term(blocks[g, c], block_rows[g, c], block_cols[g, c], block_count[g, c], source, COL_BLOCKS, True)
            return (total + lax.optimization_barrier(term.astype(jnp.bfloat16)).astype(jnp.float32), None)
        total, _ = lax.scan(add_cell, jnp.zeros((GROUP_COLS, F), jnp.float32), jnp.arange(ROW_GROUPS, dtype=jnp.int32))
        return total
    sums = lax.map(col_group, jnp.arange(COL_GROUPS, dtype=jnp.int32))
    relaid = sums.reshape(COL_GROUPS, ROW_GROUPS, NODE_DEV, F).transpose(1, 0, 2, 3).reshape(NODES, F)
    grad_nodes = (direct + relaid).astype(jnp.bfloat16)
    return (updated, grad_nodes, grad_in, grad_mid, grad_out)
```

```python
import functools
import math

import jax
import jax.numpy as jnp
from jax import lax
from jax.experimental import pallas as pl
from jax.experimental.pallas import tpu as pltpu
from jax.sharding import PartitionSpec as P

F32 = jnp.float32
BF16 = jnp.bfloat16
MESH = pl.DeviceIdType.MESH
VMEM_LIMIT = 50 * 1024 * 1024
UNROLL = 8


def in_vmem(count):
    return [pl.BlockSpec(memory_space=pltpu.VMEM)] * count


def nn(a, b):
    return lax.dot_general(a, b, (((1,), (0,)), ((), ())), preferred_element_type=F32)


def nt(a, b):
    return lax.dot_general(a, b, (((1,), (1,)), ((), ())), preferred_element_type=F32)


def tn(a, b):
    return lax.dot_general(a, b, (((0,), (0,)), ((), ())), preferred_element_type=F32)


def cell_kernel(transposed, from_ref, to_ref, count_ref, blocks_ref, src_ref, out_ref, acc):
    side = blocks_ref.shape[1]
    count = count_ref[0]
    acc[...] = jnp.zeros_like(acc)

    def body(step, carry):
        prods = []
        for u in range(UNROLL):
            s = step * UNROLL + u
            start = pl.multiple_of(from_ref[s] * side, side)
            rows = src_ref[pl.ds(start, side), :]
            block = jnp.where(s < count, blocks_ref[s], jnp.zeros((side, side), BF16))
            prods.append(tn(block, rows) if transposed else nn(block, rows))
        for u in range(UNROLL):
            s = step * UNROLL + u
            to = pl.multiple_of(to_ref[s] * side, side)
            acc[pl.ds(to, side), :] += prods[u]
        return carry

    lax.fori_loop(0, (count + UNROLL - 1) // UNROLL, body, 0)
    out_ref[...] = acc[...].astype(out_ref.dtype)


def cell_term(blocks, from_idx, to_idx, count, source, n_dst, transposed):
    slots, side, _ = blocks.shape
    feats = source.shape[1]
    smem = pl.BlockSpec(memory_space=pltpu.SMEM)
    return pl.pallas_call(
        functools.partial(cell_kernel, transposed),
        out_shape=jax.ShapeDtypeStruct((n_dst, feats), BF16),
        in_specs=[smem] * 3 + in_vmem(2),
        out_specs=in_vmem(1)[0],
        scratch_shapes=[pltpu.VMEM((n_dst, feats), F32)],
        compiler_params=pltpu.CompilerParams(vmem_limit_bytes=VMEM_LIMIT),
        cost_estimate=pl.CostEstimate(
            flops=2 * slots * side * side * feats,
            bytes_accessed=slots * side * side * 2 + 4 * n_dst * feats,
            transcendentals=0,
        ),
    )(from_idx, to_idx, count, blocks, source)


def middle_kernel(
    ncol, part, feat, cot, w_in, w_mid, w_out,
    upd, direct, rows_out, grads,
    land, joined, pre_one, back_two, act_one, act_two, gp_two, gp_one,
    send_a, recv_a, send_b, recv_b,
):
    r, c = lax.axis_index("row"), lax.axis_index("col")
    n, feats = feat.shape
    hid = w_mid.shape[0]
    half = n // 2

    barrier = pltpu.get_barrier_semaphore()
    for d in range(1, ncol):
        pl.semaphore_signal(barrier, inc=1, device_id=(r, lax.rem(c + d, ncol)), device_id_type=MESH)
    pl.semaphore_wait(barrier, ncol - 1)

    sums = []
    for d in range(1, ncol):
        peer = lax.rem(c + d, ncol)
        copy = pltpu.make_async_remote_copy(
            src_ref=part.at[pl.ds(pl.multiple_of(peer * n, n), n)],
            dst_ref=land.at[d - 1],
            send_sem=send_a.at[d - 1],
            recv_sem=recv_a.at[d - 1],
            device_id=(r, peer),
            device_id_type=MESH,
        )
        copy.start()
        sums.append(copy)

    joined[:, :feats] = feat[...]

    def early(i, carry):
        rows = pl.ds(pl.multiple_of(i * half, half), half)
        pre_one[rows, :] = nn(feat[rows, :], w_in[:feats, :])
        back_two[rows, :] = nt(cot[rows, :], w_out[...])
        return carry

    lax.fori_loop(0, 2, early, 0)

    for copy in sums:
        copy.wait()

    def network(i, carry):
        rows = pl.ds(pl.multiple_of(i * half, half), half)
        total = part[pl.ds(pl.multiple_of(c * n + i * half, half), half), :].astype(F32)
        for d in range(1, ncol):
            total = total + land[d - 1, rows, :].astype(F32)
        agg = total.astype(BF16)
        joined[rows, feats:] = agg
        one = pre_one[rows, :] + nn(agg, w_in[feats:, :])
        sig_one = jax.nn.sigmoid(one)
        a_one = (one * sig_one).astype(BF16)
        act_one[rows, :] = a_one
        pre_one[rows, :] = sig_one * (1.0 + one * (1.0 - sig_one))
        two = nn(a_one, w_mid[...])
        sig_two = jax.nn.sigmoid(two)
        act_two[rows, :] = (two * sig_two).astype(BF16)
        g_two = (back_two[rows, :] * (sig_two * (1.0 + two * (1.0 - sig_two)))).astype(BF16)
        gp_two[rows, :] = g_two
        g_one = (nt(g_two, w_mid[...]) * pre_one[rows, :]).astype(BF16)
        gp_one[rows, :] = g_one
        rows_out[pl.ds(pl.multiple_of(c * n + i * half, half), half), :] = nt(
            g_one, w_in[feats:, :]
        ).astype(BF16)
        return carry

    lax.fori_loop(0, 2, network, 0)

    gathers = []
    mine = rows_out.at[pl.ds(pl.multiple_of(c * n, n), n)]
    for d in range(1, ncol):
        copy = pltpu.make_async_remote_copy(
            src_ref=mine,
            dst_ref=mine,
            send_sem=send_b.at[d - 1],
            recv_sem=recv_b.at[d - 1],
            device_id=(r, lax.rem(c + d, ncol)),
            device_id_type=MESH,
        )
        copy.start()
        gathers.append(copy)

    def late(i, carry):
        rows = pl.ds(pl.multiple_of(i * half, half), half)
        direct[rows, :] = cot[rows, :].astype(F32) + nt(gp_one[rows, :], w_in[:feats, :])
        upd[rows, :] = (
            feat[rows, :].astype(F32) + nn(act_two[rows, :], w_out[...])
        ).astype(BF16)
        return carry

    lax.fori_loop(0, 2, late, 0)

    grads[:feats, :] = tn(cot[...], act_two[...]).astype(BF16)

    def mid_tile(i, carry):
        cols = pl.ds(pl.multiple_of(i * feats, feats), feats)
        grads[pl.ds(pl.multiple_of(feats + i * feats, feats), feats), :] = tn(
            act_one[:, cols], gp_two[...]
        ).astype(BF16)
        return carry

    lax.fori_loop(0, hid // feats, mid_tile, 0)

    def in_tile(i, carry):
        cols = pl.ds(pl.multiple_of(i * feats, feats), feats)
        grads[pl.ds(pl.multiple_of(feats + hid + i * feats, feats), feats), :] = tn(
            joined[:, cols], gp_one[...]
        ).astype(BF16)
        return carry

    lax.fori_loop(0, 2, in_tile, 0)

    for copy in gathers:
        copy.wait()


def middle(part, feat, cot, w_in, w_mid, w_out, ncol):
    n, feats = feat.shape
    hid = w_mid.shape[0]
    shape = jax.ShapeDtypeStruct
    return pl.pallas_call(
        functools.partial(middle_kernel, ncol),
        out_shape=(
            shape((n, feats), BF16),
            shape((n, feats), F32),
            shape((n * ncol, feats), BF16),
            shape((3 * feats + hid, hid), BF16),
        ),
        in_specs=in_vmem(6),
        out_specs=tuple(in_vmem(4)),
        scratch_shapes=[
            pltpu.VMEM((ncol - 1, n, feats), BF16),
            pltpu.VMEM((n, 2 * feats), BF16),
            pltpu.VMEM((n, hid), F32),
            pltpu.VMEM((n, hid), F32),
            pltpu.VMEM((n, hid), BF16),
            pltpu.VMEM((n, hid), BF16),
            pltpu.VMEM((n, hid), BF16),
            pltpu.VMEM((n, hid), BF16),
        ]
        + [pltpu.SemaphoreType.DMA((ncol - 1,))] * 4,
        compiler_params=pltpu.CompilerParams(
            collective_id=1, has_side_effects=True, vmem_limit_bytes=VMEM_LIMIT
        ),
        cost_estimate=pl.CostEstimate(
            flops=6 * n * (3 * feats + hid) * hid,
            bytes_accessed=4 * (3 * feats + hid) * hid,
            transcendentals=2 * n * hid,
        ),
    )(part, feat, cot, w_in, w_mid, w_out)


def tail_kernel(
    nrow, ncol, chunks, back, direct, grads,
    nodes, total,
    pair_land, pair_sum, chip_land, g_pair, g_half, g_col, g_colsum, g_chip,
    ps, pr, cs, cr, s0, r0, s1, r1, s2, r2, s3, r3, s4, r4, s5, r5,
):
    r, c = lax.axis_index("row"), lax.axis_index("col")
    chips = nrow // 2
    chip, core = r // 2, lax.rem(r, 2)
    other = 1 - core
    sibling = chip * 2 + other
    n = direct.shape[0]
    hid = grads.shape[1]
    width = hid // chips

    barrier = pltpu.get_barrier_semaphore()
    pl.semaphore_signal(barrier, inc=1, device_id=(sibling, c), device_id_type=MESH)
    for d in range(1, ncol):
        pl.semaphore_signal(barrier, inc=1, device_id=(r, lax.rem(c + d, ncol)), device_id_type=MESH)
    for d in range(1, chips):
        pl.semaphore_signal(
            barrier, inc=1, device_id=(lax.rem(chip + d, chips) * 2 + core, c), device_id_type=MESH
        )
    pl.semaphore_wait(barrier, ncol + chips - 1)

    def send(src, dst, ssem, rsem, device):
        copy = pltpu.make_async_remote_copy(
            src_ref=src, dst_ref=dst, send_sem=ssem, recv_sem=rsem,
            device_id=device, device_id_type=MESH,
        )
        copy.start()
        return copy

    def rows_at(start, size, unit):
        return pl.ds(pl.multiple_of(start, unit), size)

    pair = []
    for d in range(chips):
        z = lax.rem(chip + 1 + d, chips)
        pair.append(
            send(
                back.at[rows_at((z * 2 + other) * n, n, n)],
                pair_land.at[d], ps.at[d], pr.at[d], (sibling, c),
            )
        )

    offsets, halves = [], []
    at, at_half = 0, 0
    for rows in chunks:
        offsets.append(at)
        halves.append(at_half)
        at += rows
        at_half += rows // 2
    stage0 = []
    for q, rows in enumerate(chunks):
        h = rows // 2
        stage0.append(
            send(
                grads.at[rows_at(offsets[q] + other * h, h, 16)],
                g_pair.at[pl.ds(halves[q], h)], s0.at[q], r0.at[q], (sibling, c),
            )
        )

    across = []
    for d in range(chips):
        pair[d].wait()
        z = lax.rem(chip + 1 + d, chips)
        pair_sum[d] = (
            back[rows_at((z * 2 + core) * n, n, n), :].astype(F32) + pair_land[d].astype(F32)
        ).astype(BF16)
        if d < chips - 1:
            across.append(
                send(
                    pair_sum.at[d], chip_land.at[d], cs.at[d], cr.at[d], (z * 2 + core, c)
                )
            )

    stage1 = []
    for q, rows in enumerate(chunks):
        h = rows // 2
        m = h // ncol
        stage0[q].wait()
        g_half[pl.ds(halves[q], h), :] = (
            grads[rows_at(offsets[q] + core * h, h, 16), :].astype(F32)
            + g_pair[pl.ds(halves[q], h), :].astype(F32)
        ).astype(BF16)
        copies = []
        for d in range(1, ncol):
            peer = lax.rem(c + d, ncol)
            copies.append(
                send(
                    g_half.at[rows_at(halves[q] + peer * m, m, 16)],
                    g_col.at[d - 1, pl.ds(halves[q] // ncol, m)],
                    s1.at[q, d - 1], r1.at[q, d - 1], (r, peer),
                )
            )
        stage1.append(copies)

    stage2 = []
    for q, rows in enumerate(chunks):
        h = rows // 2
        m = h // ncol
        base = halves[q] // ncol
        for copy in stage1[q]:
            copy.wait()
        value = g_half[rows_at(halves[q] + c * m, m, 16), :].astype(F32)
        for d in range(1, ncol):
            value = value + g_col[d - 1, pl.ds(base, m), :].astype(F32)
        g_colsum[pl.ds(base, m), :] = value.astype(BF16)
        copies = []
        for d in range(1, chips):
            z = lax.rem(chip + d, chips)
            copies.append(
                send(
                    g_colsum.at[pl.ds(base, m), rows_at(z * width, width, width)],
                    g_chip.at[d - 1, pl.ds(base, m)],
                    s2.at[q, d - 1], r2.at[q, d - 1], (z * 2 + core, c),
                )
            )
        stage2.append(copies)

    stage3 = []
    for q, rows in enumerate(chunks):
        h = rows // 2
        m = h // ncol
        base = halves[q] // ncol
        for copy in stage2[q]:
            copy.wait()
        columns = rows_at(chip * width, width, width)
        value = g_colsum[pl.ds(base, m), columns].astype(F32)
        for d in range(1, chips):
            value = value + g_chip[d - 1, pl.ds(base, m), :].astype(F32)
        spot = total.at[rows_at(offsets[q] + core * h + c * m, m, 16), columns]
        spot[...] = value.astype(BF16)
        copies = []
        for d in range(1, chips):
            z = lax.rem(chip + d, chips)
            copies.append(send(spot, spot, s3.at[q, d - 1], r3.at[q, d - 1], (z * 2 + core, c)))
        stage3.append(copies)

    stage4 = []
    for q, rows in enumerate(chunks):
        h = rows // 2
        m = h // ncol
        for copy in stage3[q]:
            copy.wait()
        spot = total.at[rows_at(offsets[q] + core * h + c * m, m, 16)]
        copies = []
        for d in range(1, ncol):
            copies.append(
                send(spot, spot, s4.at[q, d - 1], r4.at[q, d - 1], (r, lax.rem(c + d, ncol)))
            )
        stage4.append(copies)

    for copy in across:
        copy.wait()
    value = direct[...] + pair_sum[chips - 1].astype(F32)
    for d in range(chips - 1):
        value = value + chip_land[d].astype(F32)
    nodes[...] = value.astype(BF16)

    stage5 = []
    for q, rows in enumerate(chunks):
        h = rows // 2
        for copy in stage4[q]:
            copy.wait()
        spot = total.at[rows_at(offsets[q] + core * h, h, 16)]
        stage5.append(send(spot, spot, s5.at[q], r5.at[q], (sibling, c)))
    for copy in stage5:
        copy.wait()


def tail(back, direct, grads, nrow, ncol):
    n, feats = direct.shape
    rows, hid = grads.shape
    chips = nrow // 2
    unit = 32 * ncol
    first = rows // 3 // unit * unit
    chunks = (first, first, rows - 2 * first)
    parts = len(chunks)
    shape = jax.ShapeDtypeStruct
    dma = pltpu.SemaphoreType.DMA
    return pl.pallas_call(
        functools.partial(tail_kernel, nrow, ncol, chunks),
        out_shape=(shape((n, feats), BF16), shape((rows, hid), BF16)),
        in_specs=in_vmem(3),
        out_specs=tuple(in_vmem(2)),
        scratch_shapes=[
            pltpu.VMEM((chips, n, feats), BF16),
            pltpu.VMEM((chips, n, feats), BF16),
            pltpu.VMEM((chips - 1, n, feats), BF16),
            pltpu.VMEM((rows // 2, hid), BF16),
            pltpu.VMEM((rows // 2, hid), BF16),
            pltpu.VMEM((ncol - 1, rows // 2 // ncol, hid), BF16),
            pltpu.VMEM((rows // 2 // ncol, hid), BF16),
            pltpu.VMEM((chips - 1, rows // 2 // ncol, hid // chips), BF16),
        ]
        + [dma((chips,))] * 2
        + [dma((chips - 1,))] * 2
        + [dma((parts,))] * 2
        + [dma((parts, ncol - 1))] * 2
        + [dma((parts, chips - 1))] * 4
        + [dma((parts, ncol - 1))] * 2
        + [dma((parts,))] * 2,
        compiler_params=pltpu.CompilerParams(
            collective_id=2, has_side_effects=True, vmem_limit_bytes=VMEM_LIMIT
        ),
    )(back, direct, grads)


def shards(features, blocks, block_rows, block_cols, block_count, w_in, w_mid, w_out, cotangent):
    nrow, ncol = lax.axis_size("row"), lax.axis_size("col")
    node_dev, feats = features.shape
    hid = w_mid.shape[0]
    cell_blocks = blocks[0, 0]
    rows_here = block_rows[0, 0]
    cols_here = block_cols[0, 0]
    count = block_count[0]
    column_feats = lax.all_gather(features, "row", axis=0, tiled=True)
    part = cell_term(
        cell_blocks, cols_here, rows_here, count, column_feats, node_dev * ncol, False
    )
    updated, direct, row_grads, grads = middle(
        part, features, cotangent, w_in, w_mid, w_out, ncol
    )
    back = cell_term(
        cell_blocks, rows_here, cols_here, count, row_grads, node_dev * nrow, True
    )
    grad_nodes, total = tail(back, direct, grads, nrow, ncol)
    ratio = 1.0 / math.sqrt(node_dev * nrow * ncol)
    total = total.astype(F32) * ratio
    return (
        updated,
        grad_nodes,
        total[feats + hid :],
        total[feats : feats + hid],
        total[:feats].T,
    )


def solution(mesh):
    placed = (
        P(("row", "col"), None),
        P("row", "col", None, None, None),
        P("row", "col", None),
        P("row", "col", None),
        P("row", "col"),
        P(),
        P(),
        P(),
        P(("row", "col"), None),
    )
    return jax.shard_map(
        shards,
        mesh=mesh,
        in_specs=placed,
        out_specs=(P(("row", "col"), None), P(("row", "col"), None), P(), P(), P()),
        check_vma=False,
    )
```

```python
import functools
import math

import jax
import jax.numpy as jnp
from jax import lax
from jax.experimental import pallas as pl
from jax.experimental.pallas import tpu as pltpu
from jax.sharding import PartitionSpec as P

F32 = jnp.float32
BF16 = jnp.bfloat16
MESH = pl.DeviceIdType.MESH
VMEM_LIMIT = 50 * 1024 * 1024
UNROLL = 8


def in_vmem(count):
    return [pl.BlockSpec(memory_space=pltpu.VMEM)] * count


def nn(a, b):
    return lax.dot_general(a, b, (((1,), (0,)), ((), ())), preferred_element_type=F32)


def nt(a, b):
    return lax.dot_general(a, b, (((1,), (1,)), ((), ())), preferred_element_type=F32)


def tn(a, b):
    return lax.dot_general(a, b, (((0,), (0,)), ((), ())), preferred_element_type=F32)


def cell_kernel(transposed, from_ref, to_ref, count_ref, blocks_ref, src_ref, out_ref, acc):
    side = blocks_ref.shape[1]
    count = count_ref[0]
    acc[...] = jnp.zeros_like(acc)

    def body(step, carry):
        prods = []
        for u in range(UNROLL):
            s = step * UNROLL + u
            start = pl.multiple_of(from_ref[s] * side, side)
            rows = src_ref[pl.ds(start, side), :]
            block = jnp.where(s < count, blocks_ref[s], jnp.zeros((side, side), BF16))
            prods.append(tn(block, rows) if transposed else nn(block, rows))
        for u in range(UNROLL):
            s = step * UNROLL + u
            to = pl.multiple_of(to_ref[s] * side, side)
            acc[pl.ds(to, side), :] += prods[u]
        return carry

    lax.fori_loop(0, (count + UNROLL - 1) // UNROLL, body, 0)
    out_ref[...] = acc[...].astype(out_ref.dtype)


def cell_term(blocks, from_idx, to_idx, count, source, n_dst, transposed):
    slots, side, _ = blocks.shape
    feats = source.shape[1]
    smem = pl.BlockSpec(memory_space=pltpu.SMEM)
    return pl.pallas_call(
        functools.partial(cell_kernel, transposed),
        out_shape=jax.ShapeDtypeStruct((n_dst, feats), BF16),
        in_specs=[smem] * 3 + in_vmem(2),
        out_specs=in_vmem(1)[0],
        scratch_shapes=[pltpu.VMEM((n_dst, feats), F32)],
        compiler_params=pltpu.CompilerParams(vmem_limit_bytes=VMEM_LIMIT),
        cost_estimate=pl.CostEstimate(
            flops=2 * slots * side * side * feats,
            bytes_accessed=slots * side * side * 2 + 4 * n_dst * feats,
            transcendentals=0,
        ),
    )(from_idx, to_idx, count, blocks, source)


def chunk_list(feats, hid):
    mid = hid // 2
    return (
        (0, feats),
        (feats, mid),
        (feats + mid, mid),
        (feats + hid, feats),
        (2 * feats + hid, feats),
    )


def middle_kernel(
    ncol, part, feat, cot, w_in, w_mid, w_out,
    upd, direct, rows_out, g_half,
    grads, g_pair, land, joined, pre_one, back_two, act_one, act_two, gp_two, gp_one,
    send_a, recv_a, send_b, recv_b, send_c, recv_c,
):
    r, c = lax.axis_index("row"), lax.axis_index("col")
    n, feats = feat.shape
    hid = w_mid.shape[0]
    half = n // 2
    core = lax.rem(r, 2)
    sibling = r + 1 - 2 * core

    barrier = pltpu.get_barrier_semaphore()
    pl.semaphore_signal(barrier, inc=1, device_id=(sibling, c), device_id_type=MESH)
    for d in range(1, ncol):
        pl.semaphore_signal(barrier, inc=1, device_id=(r, lax.rem(c + d, ncol)), device_id_type=MESH)
    pl.semaphore_wait(barrier, ncol)

    sums = []
    for i in range(2):
        sums.append([])
        for d in range(1, ncol):
            peer = lax.rem(c + d, ncol)
            copy = pltpu.make_async_remote_copy(
                src_ref=part.at[pl.ds(pl.multiple_of(peer * n + i * half, half), half)],
                dst_ref=land.at[d - 1, pl.ds(i * half, half)],
                send_sem=send_a.at[i, d - 1],
                recv_sem=recv_a.at[i, d - 1],
                device_id=(r, peer),
                device_id_type=MESH,
            )
            copy.start()
            sums[i].append(copy)

    joined[:, :feats] = feat[...]

    def early(i, carry):
        rows = pl.ds(pl.multiple_of(i * half, half), half)
        pre_one[rows, :] = nn(feat[rows, :], w_in[:feats, :])
        back_two[rows, :] = nt(cot[rows, :], w_out[...])
        return carry

    lax.fori_loop(0, 2, early, 0)

    gathers = []
    for i in range(2):
        for copy in sums[i]:
            copy.wait()
        rows = pl.ds(i * half, half)
        total = part[pl.ds(pl.multiple_of(c * n + i * half, half), half), :].astype(F32)
        for d in range(1, ncol):
            total = total + land[d - 1, rows, :].astype(F32)
        agg = total.astype(BF16)
        joined[rows, feats:] = agg
        one = pre_one[rows, :] + nn(agg, w_in[feats:, :])
        sig_one = jax.nn.sigmoid(one)
        a_one = (one * sig_one).astype(BF16)
        act_one[rows, :] = a_one
        pre_one[rows, :] = sig_one * (1.0 + one * (1.0 - sig_one))
        two = nn(a_one, w_mid[...])
        sig_two = jax.nn.sigmoid(two)
        act_two[rows, :] = (two * sig_two).astype(BF16)
        g_two = (back_two[rows, :] * (sig_two * (1.0 + two * (1.0 - sig_two)))).astype(BF16)
        gp_two[rows, :] = g_two
        g_one = (nt(g_two, w_mid[...]) * pre_one[rows, :]).astype(BF16)
        gp_one[rows, :] = g_one
        rows_out[pl.ds(pl.multiple_of(c * n + i * half, half), half), :] = nt(
            g_one, w_in[feats:, :]
        ).astype(BF16)
        mine = rows_out.at[pl.ds(pl.multiple_of(c * n + i * half, half), half)]
        for d in range(1, ncol):
            copy = pltpu.make_async_remote_copy(
                src_ref=mine,
                dst_ref=mine,
                send_sem=send_b.at[i, d - 1],
                recv_sem=recv_b.at[i, d - 1],
                device_id=(r, lax.rem(c + d, ncol)),
                device_id_type=MESH,
            )
            copy.start()
            gathers.append(copy)

    pairs = []

    def trade(q):
        at, rows = chunk_list(feats, hid)[q]
        h = rows // 2
        copy = pltpu.make_async_remote_copy(
            src_ref=grads.at[pl.ds(pl.multiple_of(at + (1 - core) * h, h), h)],
            dst_ref=g_pair.at[pl.ds(at // 2, h)],
            send_sem=send_c.at[q],
            recv_sem=recv_c.at[q],
            device_id=(sibling, c),
            device_id_type=MESH,
        )
        copy.start()
        pairs.append(copy)

    grads[:feats, :] = tn(cot[...], act_two[...]).astype(BF16)
    trade(0)

    def mid_tile(i, carry):
        cols = pl.ds(pl.multiple_of(i * feats, feats), feats)
        grads[pl.ds(pl.multiple_of(feats + i * feats, feats), feats), :] = tn(
            act_one[:, cols], gp_two[...]
        ).astype(BF16)
        return carry

    lax.fori_loop(0, hid // feats, mid_tile, 0)
    trade(1)
    trade(2)

    def in_tile(i, carry):
        cols = pl.ds(pl.multiple_of(i * feats, feats), feats)
        grads[pl.ds(pl.multiple_of(feats + hid + i * feats, feats), feats), :] = tn(
            joined[:, cols], gp_one[...]
        ).astype(BF16)
        return carry

    lax.fori_loop(0, 2, in_tile, 0)
    trade(3)
    trade(4)

    def late(i, carry):
        rows = pl.ds(pl.multiple_of(i * half, half), half)
        direct[rows, :] = cot[rows, :].astype(F32) + nt(gp_one[rows, :], w_in[:feats, :])
        upd[rows, :] = (
            feat[rows, :].astype(F32) + nn(act_two[rows, :], w_out[...])
        ).astype(BF16)
        return carry

    lax.fori_loop(0, 2, late, 0)

    for q, (at, rows) in enumerate(chunk_list(feats, hid)):
        h = rows // 2
        pairs[q].wait()
        g_half[pl.ds(at // 2, h), :] = (
            grads[pl.ds(pl.multiple_of(at + core * h, h), h), :].astype(F32)
            + g_pair[pl.ds(at // 2, h), :].astype(F32)
        ).astype(BF16)

    for copy in gathers:
        copy.wait()


def middle(part, feat, cot, w_in, w_mid, w_out, ncol):
    n, feats = feat.shape
    hid = w_mid.shape[0]
    shape = jax.ShapeDtypeStruct
    return pl.pallas_call(
        functools.partial(middle_kernel, ncol),
        out_shape=(
            shape((n, feats), BF16),
            shape((n, feats), F32),
            shape((n * ncol, feats), BF16),
            shape(((3 * feats + hid) // 2, hid), BF16),
        ),
        in_specs=in_vmem(6),
        out_specs=tuple(in_vmem(4)),
        scratch_shapes=[
            pltpu.VMEM((3 * feats + hid, hid), BF16),
            pltpu.VMEM(((3 * feats + hid) // 2, hid), BF16),
            pltpu.VMEM((ncol - 1, n, feats), BF16),
            pltpu.VMEM((n, 2 * feats), BF16),
            pltpu.VMEM((n, hid), F32),
            pltpu.VMEM((n, hid), F32),
            pltpu.VMEM((n, hid), BF16),
            pltpu.VMEM((n, hid), BF16),
            pltpu.VMEM((n, hid), BF16),
            pltpu.VMEM((n, hid), BF16),
        ]
        + [pltpu.SemaphoreType.DMA((2, ncol - 1))] * 4
        + [pltpu.SemaphoreType.DMA((5,))] * 2,
        compiler_params=pltpu.CompilerParams(
            collective_id=1, has_side_effects=True, vmem_limit_bytes=VMEM_LIMIT
        ),
        cost_estimate=pl.CostEstimate(
            flops=6 * n * (3 * feats + hid) * hid,
            bytes_accessed=4 * (3 * feats + hid) * hid,
            transcendentals=2 * n * hid,
        ),
    )(part, feat, cot, w_in, w_mid, w_out)


def tail_kernel(
    nrow, ncol, back, direct, g_half,
    nodes, t_out, t_mid, t_in,
    pair_land, pair_sum, chip_land, g_col, g_colsum, g_chip, g_first,
    ps, pr, cs, cr, s1, r1, s2, r2, s3, r3, s4, r4, s5, r5,
):
    r, c = lax.axis_index("row"), lax.axis_index("col")
    chips = nrow // 2
    chip, core = r // 2, lax.rem(r, 2)
    other = 1 - core
    sibling = chip * 2 + other
    n, feats = direct.shape
    hid = g_half.shape[1]
    width = hid // chips
    chunks = chunk_list(feats, hid)
    homes = (
        (g_first, 0), (t_mid, 0), (t_mid, hid // 2), (t_in, 0), (t_in, feats)
    )

    barrier = pltpu.get_barrier_semaphore()
    pl.semaphore_signal(barrier, inc=1, device_id=(sibling, c), device_id_type=MESH)
    for d in range(1, ncol):
        pl.semaphore_signal(barrier, inc=1, device_id=(r, lax.rem(c + d, ncol)), device_id_type=MESH)
    for d in range(1, chips):
        pl.semaphore_signal(
            barrier, inc=1, device_id=(lax.rem(chip + d, chips) * 2 + core, c), device_id_type=MESH
        )
    pl.semaphore_wait(barrier, ncol + chips - 1)

    def send(src, dst, ssem, rsem, device):
        copy = pltpu.make_async_remote_copy(
            src_ref=src, dst_ref=dst, send_sem=ssem, recv_sem=rsem,
            device_id=device, device_id_type=MESH,
        )
        copy.start()
        return copy

    def rows_at(start, size, unit):
        return pl.ds(pl.multiple_of(start, unit), size)

    pair = []
    for d in range(chips):
        z = lax.rem(chip + 1 + d, chips)
        pair.append(
            send(
                back.at[rows_at((z * 2 + other) * n, n, n)],
                pair_land.at[d], ps.at[d], pr.at[d], (sibling, c),
            )
        )

    stage1 = []
    for q, (at, rows) in enumerate(chunks):
        m = rows // 2 // ncol
        copies = []
        for d in range(1, ncol):
            peer = lax.rem(c + d, ncol)
            copies.append(
                send(
                    g_half.at[rows_at(at // 2 + peer * m, m, 16)],
                    g_col.at[d - 1, pl.ds(at // 2 // ncol, m)],
                    s1.at[q, d - 1], r1.at[q, d - 1], (r, peer),
                )
            )
        stage1.append(copies)

    across = []

    def across_send(d):
        z = lax.rem(chip + 1 + d, chips)
        across.append(
            send(pair_sum.at[d], chip_land.at[d], cs.at[d], cr.at[d], (z * 2 + core, c))
        )

    late = chips // 4
    for d in range(chips):
        pair[d].wait()
        z = lax.rem(chip + 1 + d, chips)
        pair_sum[d] = (
            back[rows_at((z * 2 + core) * n, n, n), :].astype(F32) + pair_land[d].astype(F32)
        ).astype(BF16)
        if d < chips - 1 - late:
            across_send(d)

    stage2, stage3, stage4, stage5 = [], [], [], []

    def over_chips(q):
        at, rows = chunks[q]
        m = rows // 2 // ncol
        base = at // 2 // ncol
        for copy in stage1[q]:
            copy.wait()
        value = g_half[rows_at(at // 2 + c * m, m, 16), :].astype(F32)
        for d in range(1, ncol):
            value = value + g_col[d - 1, pl.ds(base, m), :].astype(F32)
        g_colsum[pl.ds(base, m), :] = value.astype(BF16)
        copies = []
        for d in range(1, chips):
            z = lax.rem(chip + d, chips)
            copies.append(
                send(
                    g_colsum.at[pl.ds(base, m), rows_at(z * width, width, width)],
                    g_chip.at[d - 1, pl.ds(base, m)],
                    s2.at[q, d - 1], r2.at[q, d - 1], (z * 2 + core, c),
                )
            )
        stage2.append(copies)

    def back_over_chips(q):
        at, rows = chunks[q]
        home, first = homes[q]
        h = rows // 2
        m = h // ncol
        base = at // 2 // ncol
        for copy in stage2[q]:
            copy.wait()
        columns = rows_at(chip * width, width, width)
        value = g_colsum[pl.ds(base, m), columns].astype(F32)
        for d in range(1, chips):
            value = value + g_chip[d - 1, pl.ds(base, m), :].astype(F32)
        spot = home.at[rows_at(first + core * h + c * m, m, 16), columns]
        spot[...] = value.astype(BF16)
        copies = []
        for d in range(1, chips):
            z = lax.rem(chip + d, chips)
            copies.append(send(spot, spot, s3.at[q, d - 1], r3.at[q, d - 1], (z * 2 + core, c)))
        stage3.append(copies)

    def back_over_col(q):
        _, rows = chunks[q]
        home, first = homes[q]
        h = rows // 2
        m = h // ncol
        for copy in stage3[q]:
            copy.wait()
        spot = home.at[rows_at(first + core * h + c * m, m, 16)]
        copies = []
        for d in range(1, ncol):
            copies.append(
                send(spot, spot, s4.at[q, d - 1], r4.at[q, d - 1], (r, lax.rem(c + d, ncol)))
            )
        stage4.append(copies)

    def back_to_pair(q):
        _, rows = chunks[q]
        home, first = homes[q]
        h = rows // 2
        for copy in stage4[q]:
            copy.wait()
        spot = home.at[rows_at(first + core * h, h, 16)]
        stage5.append(send(spot, spot, s5.at[q], r5.at[q], (sibling, c)))

    parts = len(chunks)
    for step in range(parts + 2):
        if step < parts:
            over_chips(step)
        if 1 <= step <= parts:
            back_over_chips(step - 1)
        if step >= 2:
            back_over_col(step - 2)
    for d in range(chips - 1 - late, chips - 1):
        across_send(d)
    for q in range(parts - 1):
        back_to_pair(q)
    stage5[0].wait()
    t_out[...] = jnp.transpose(g_first[...].astype(F32)).astype(BF16)
    for copy in across:
        copy.wait()
    value = direct[...] + pair_sum[chips - 1].astype(F32)
    for d in range(chips - 1):
        value = value + chip_land[d].astype(F32)
    nodes[...] = value.astype(BF16)
    back_to_pair(parts - 1)
    for copy in stage5[1:]:
        copy.wait()


def tail(back, direct, g_half, nrow, ncol):
    n, feats = direct.shape
    rows, hid = g_half.shape
    chips = nrow // 2
    parts = len(chunk_list(feats, hid))
    shape = jax.ShapeDtypeStruct
    dma = pltpu.SemaphoreType.DMA
    return pl.pallas_call(
        functools.partial(tail_kernel, nrow, ncol),
        out_shape=(
            shape((n, feats), BF16),
            shape((hid, feats), BF16),
            shape((hid, hid), BF16),
            shape((2 * feats, hid), BF16),
        ),
        in_specs=in_vmem(3),
        out_specs=tuple(in_vmem(4)),
        scratch_shapes=[
            pltpu.VMEM((chips, n, feats), BF16),
            pltpu.VMEM((chips, n, feats), BF16),
            pltpu.VMEM((chips - 1, n, feats), BF16),
            pltpu.VMEM((ncol - 1, rows // ncol, hid), BF16),
            pltpu.VMEM((rows // ncol, hid), BF16),
            pltpu.VMEM((chips - 1, rows // ncol, hid // chips), BF16),
            pltpu.VMEM((feats, hid), BF16),
        ]
        + [dma((chips,))] * 2
        + [dma((chips - 1,))] * 2
        + [dma((parts, ncol - 1))] * 2
        + [dma((parts, chips - 1))] * 4
        + [dma((parts, ncol - 1))] * 2
        + [dma((parts,))] * 2,
        compiler_params=pltpu.CompilerParams(
            collective_id=2, has_side_effects=True, vmem_limit_bytes=VMEM_LIMIT
        ),
    )(back, direct, g_half)


def gather_kernel(nrow, feat, out, own_sem, ss, sr, rs, rr, ls, lr, fs, fr):
    r, c = lax.axis_index("row"), lax.axis_index("col")
    chips = nrow // 2
    chip, core = r // 2, lax.rem(r, 2)
    sibling = chip * 2 + 1 - core
    n = feat.shape[0]
    up, down = chip < chips - 1, chip > 0
    above = lax.rem(chip + 1, chips) * 2 + core
    below = lax.rem(chip + chips - 1, chips) * 2 + core

    def spot(device):
        return out.at[pl.ds(pl.multiple_of(device * n, n), n)]

    def remote(src, dst, ssem, rsem, device):
        return pltpu.make_async_remote_copy(
            src_ref=src, dst_ref=dst, send_sem=ssem, recv_sem=rsem,
            device_id=(device, c), device_id_type=MESH,
        )

    own = pltpu.make_async_copy(feat, spot(r), own_sem)
    own.start()
    barrier = pltpu.get_barrier_semaphore()
    pl.semaphore_signal(barrier, inc=1, device_id=(sibling, c), device_id_type=MESH)

    @pl.when(up)
    def _():
        pl.semaphore_signal(barrier, inc=1, device_id=(above, c), device_id_type=MESH)

    @pl.when(down)
    def _():
        pl.semaphore_signal(barrier, inc=1, device_id=(below, c), device_id_type=MESH)

    pl.semaphore_wait(barrier, 1 + up.astype(jnp.int32) + down.astype(jnp.int32))

    @pl.when(up)
    def _():
        remote(feat, spot(r), rs.at[0], rr.at[0], above).start()

    @pl.when(down)
    def _():
        remote(feat, spot(r), ls.at[0], lr.at[0], below).start()

    near = remote(feat, spot(r), ss, sr, sibling)
    near.start()

    for k in range(1, chips):
        @pl.when(chip >= k)
        def _():
            source = spot(lax.rem(chip - k + chips, chips) * 2 + core)
            remote(source, source, rs.at[k - 1], rr.at[k - 1], below).wait_recv()

            @pl.when(up)
            def _():
                remote(source, source, rs.at[k], rr.at[k], above).start()

            remote(source, source, fs.at[0, k - 1], fr.at[0, k - 1], sibling).start()

        @pl.when(chip + k < chips)
        def _():
            source = spot(lax.rem(chip + k, chips) * 2 + core)
            remote(source, source, ls.at[k - 1], lr.at[k - 1], above).wait_recv()

            @pl.when(down)
            def _():
                remote(source, source, ls.at[k], lr.at[k], below).start()

            remote(source, source, fs.at[1, k - 1], fr.at[1, k - 1], sibling).start()

    own.wait()
    near.wait()
    for k in range(chips):
        @pl.when(up & (chip >= k))
        def _():
            remote(feat, spot(r), rs.at[k], rr.at[k], above).wait_send()

        @pl.when(down & (chip + k < chips))
        def _():
            remote(feat, spot(r), ls.at[k], lr.at[k], below).wait_send()

        if k:
            @pl.when(chip >= k)
            def _():
                source = spot(lax.rem(chip - k + chips, chips) * 2 + core)
                landed = spot(lax.rem(chip - k + chips, chips) * 2 + 1 - core)
                remote(source, landed, fs.at[0, k - 1], fr.at[0, k - 1], sibling).wait()

            @pl.when(chip + k < chips)
            def _():
                source = spot(lax.rem(chip + k, chips) * 2 + core)
                landed = spot(lax.rem(chip + k, chips) * 2 + 1 - core)
                remote(source, landed, fs.at[1, k - 1], fr.at[1, k - 1], sibling).wait()


def gather(feat, nrow):
    n, feats = feat.shape
    chips = nrow // 2
    dma = pltpu.SemaphoreType.DMA
    return pl.pallas_call(
        functools.partial(gather_kernel, nrow),
        out_shape=jax.ShapeDtypeStruct((n * nrow, feats), BF16),
        in_specs=in_vmem(1),
        out_specs=in_vmem(1)[0],
        scratch_shapes=[dma] * 3 + [dma((chips,))] * 4 + [dma((2, chips - 1))] * 2,
        compiler_params=pltpu.CompilerParams(
            collective_id=3, has_side_effects=True, vmem_limit_bytes=VMEM_LIMIT
        ),
    )(feat)


def shards(features, blocks, block_rows, block_cols, block_count, w_in, w_mid, w_out, cotangent):
    nrow, ncol = lax.axis_size("row"), lax.axis_size("col")
    node_dev, feats = features.shape
    hid = w_mid.shape[0]
    cell_blocks = blocks[0, 0]
    rows_here = block_rows[0, 0]
    cols_here = block_cols[0, 0]
    count = block_count[0]
    column_feats = gather(features, nrow)
    part = cell_term(
        cell_blocks, cols_here, rows_here, count, column_feats, node_dev * ncol, False
    )
    updated, direct, row_grads, grads = middle(
        part, features, cotangent, w_in, w_mid, w_out, ncol
    )
    back = cell_term(
        cell_blocks, rows_here, cols_here, count, row_grads, node_dev * nrow, True
    )
    grad_nodes, sum_out, sum_mid, sum_in = tail(back, direct, grads, nrow, ncol)
    ratio = 1.0 / math.sqrt(node_dev * nrow * ncol)
    return (
        updated,
        grad_nodes,
        sum_in.astype(F32) * ratio,
        sum_mid.astype(F32) * ratio,
        sum_out.astype(F32) * ratio,
    )


def solution(mesh):
    placed = (
        P(("row", "col"), None),
        P("row", "col", None, None, None),
        P("row", "col", None),
        P("row", "col", None),
        P("row", "col"),
        P(),
        P(),
        P(),
        P(("row", "col"), None),
    )
    return jax.shard_map(
        shards,
        mesh=mesh,
        in_specs=placed,
        out_specs=(P(("row", "col"), None), P(("row", "col"), None), P(), P(), P()),
        check_vma=False,
    )
```

```python
import functools
import math

import jax
import jax.numpy as jnp
from jax import lax
from jax.experimental import pallas as pl
from jax.experimental.pallas import tpu as pltpu
from jax.sharding import PartitionSpec as P

F32 = jnp.float32
BF16 = jnp.bfloat16
MESH = pl.DeviceIdType.MESH
VMEM_LIMIT = 50 * 1024 * 1024
UNROLL = 8


def in_vmem(count):
    return [pl.BlockSpec(memory_space=pltpu.VMEM)] * count


def nn(a, b):
    return lax.dot_general(a, b, (((1,), (0,)), ((), ())), preferred_element_type=F32)


def nt(a, b):
    return lax.dot_general(a, b, (((1,), (1,)), ((), ())), preferred_element_type=F32)


def tn(a, b):
    return lax.dot_general(a, b, (((0,), (0,)), ((), ())), preferred_element_type=F32)


def cell_kernel(transposed, from_ref, to_ref, count_ref, blocks_ref, src_ref, out_ref, acc):
    side = blocks_ref.shape[1]
    count = count_ref[0]
    acc[...] = jnp.zeros_like(acc)

    def body(step, carry):
        prods = []
        for u in range(UNROLL):
            s = step * UNROLL + u
            start = pl.multiple_of(from_ref[s] * side, side)
            rows = src_ref[pl.ds(start, side), :]
            block = jnp.where(s < count, blocks_ref[s], jnp.zeros((side, side), BF16))
            prods.append(tn(block, rows) if transposed else nn(block, rows))
        for u in range(UNROLL):
            s = step * UNROLL + u
            to = pl.multiple_of(to_ref[s] * side, side)
            acc[pl.ds(to, side), :] += prods[u]
        return carry

    lax.fori_loop(0, (count + UNROLL - 1) // UNROLL, body, 0)
    out_ref[...] = acc[...].astype(out_ref.dtype)


def cell_term(blocks, from_idx, to_idx, count, source, n_dst, transposed):
    slots, side, _ = blocks.shape
    feats = source.shape[1]
    smem = pl.BlockSpec(memory_space=pltpu.SMEM)
    return pl.pallas_call(
        functools.partial(cell_kernel, transposed),
        out_shape=jax.ShapeDtypeStruct((n_dst, feats), BF16),
        in_specs=[smem] * 3 + in_vmem(2),
        out_specs=in_vmem(1)[0],
        scratch_shapes=[pltpu.VMEM((n_dst, feats), F32)],
        compiler_params=pltpu.CompilerParams(vmem_limit_bytes=VMEM_LIMIT),
        cost_estimate=pl.CostEstimate(
            flops=2 * slots * side * side * feats,
            bytes_accessed=slots * side * side * 2 + 4 * n_dst * feats,
            transcendentals=0,
        ),
    )(from_idx, to_idx, count, blocks, source)


def chunk_list(feats, hid):
    mid = hid // 2
    return (
        (0, feats),
        (feats, mid),
        (feats + mid, mid),
        (feats + hid, feats),
        (2 * feats + hid, feats),
    )


def middle_kernel(
    ncol, part, feat, cot, w_in, w_mid, w_out,
    upd, direct, rows_out, g_half,
    grads, g_pair, land, joined, pre_one, back_two, act_one, act_two, gp_two, gp_one,
    send_a, recv_a, send_b, recv_b, send_c, recv_c,
):
    r, c = lax.axis_index("row"), lax.axis_index("col")
    n, feats = feat.shape
    hid = w_mid.shape[0]
    half = n // 2
    core = lax.rem(r, 2)
    sibling = r + 1 - 2 * core

    barrier = pltpu.get_barrier_semaphore()
    pl.semaphore_signal(barrier, inc=1, device_id=(sibling, c), device_id_type=MESH)
    for d in range(1, ncol):
        pl.semaphore_signal(barrier, inc=1, device_id=(r, lax.rem(c + d, ncol)), device_id_type=MESH)
    pl.semaphore_wait(barrier, ncol)

    sums = []
    for i in range(2):
        sums.append([])
        for d in range(1, ncol):
            peer = lax.rem(c + d, ncol)
            copy = pltpu.make_async_remote_copy(
                src_ref=part.at[pl.ds(pl.multiple_of(peer * n + i * half, half), half)],
                dst_ref=land.at[d - 1, pl.ds(i * half, half)],
                send_sem=send_a.at[i, d - 1],
                recv_sem=recv_a.at[i, d - 1],
                device_id=(r, peer),
                device_id_type=MESH,
            )
            copy.start()
            sums[i].append(copy)

    joined[:, :feats] = feat[...]

    def early(i, carry):
        rows = pl.ds(pl.multiple_of(i * half, half), half)
        pre_one[rows, :] = nn(feat[rows, :], w_in[:feats, :])
        back_two[rows, :] = nt(cot[rows, :], w_out[...])
        return carry

    lax.fori_loop(0, 2, early, 0)

    gathers = []
    for i in range(2):
        for copy in sums[i]:
            copy.wait()
        rows = pl.ds(i * half, half)
        total = part[pl.ds(pl.multiple_of(c * n + i * half, half), half), :].astype(F32)
        for d in range(1, ncol):
            total = total + land[d - 1, rows, :].astype(F32)
        agg = total.astype(BF16)
        joined[rows, feats:] = agg
        one = pre_one[rows, :] + nn(agg, w_in[feats:, :])
        sig_one = jax.nn.sigmoid(one)
        a_one = (one * sig_one).astype(BF16)
        act_one[rows, :] = a_one
        pre_one[rows, :] = sig_one * (1.0 + one * (1.0 - sig_one))
        two = nn(a_one, w_mid[...])
        sig_two = jax.nn.sigmoid(two)
        act_two[rows, :] = (two * sig_two).astype(BF16)
        g_two = (back_two[rows, :] * (sig_two * (1.0 + two * (1.0 - sig_two)))).astype(BF16)
        gp_two[rows, :] = g_two
        g_one = (nt(g_two, w_mid[...]) * pre_one[rows, :]).astype(BF16)
        gp_one[rows, :] = g_one
        rows_out[pl.ds(pl.multiple_of(c * n + i * half, half), half), :] = nt(
            g_one, w_in[feats:, :]
        ).astype(BF16)
        mine = rows_out.at[pl.ds(pl.multiple_of(c * n + i * half, half), half)]
        for d in range(1, ncol):
            copy = pltpu.make_async_remote_copy(
                src_ref=mine,
                dst_ref=mine,
                send_sem=send_b.at[i, d - 1],
                recv_sem=recv_b.at[i, d - 1],
                device_id=(r, lax.rem(c + d, ncol)),
                device_id_type=MESH,
            )
            copy.start()
            gathers.append(copy)

    pairs = []

    def trade(q):
        at, rows = chunk_list(feats, hid)[q]
        h = rows // 2
        copy = pltpu.make_async_remote_copy(
            src_ref=grads.at[pl.ds(pl.multiple_of(at + (1 - core) * h, h), h)],
            dst_ref=g_pair.at[pl.ds(at // 2, h)],
            send_sem=send_c.at[q],
            recv_sem=recv_c.at[q],
            device_id=(sibling, c),
            device_id_type=MESH,
        )
        copy.start()
        pairs.append(copy)

    grads[:feats, :] = tn(cot[...], act_two[...]).astype(BF16)
    trade(0)

    def mid_tile(i, carry):
        cols = pl.ds(pl.multiple_of(i * feats, feats), feats)
        grads[pl.ds(pl.multiple_of(feats + i * feats, feats), feats), :] = tn(
            act_one[:, cols], gp_two[...]
        ).astype(BF16)
        return carry

    lax.fori_loop(0, hid // feats, mid_tile, 0)
    trade(1)
    trade(2)

    def in_tile(i, carry):
        cols = pl.ds(pl.multiple_of(i * feats, feats), feats)
        grads[pl.ds(pl.multiple_of(feats + hid + i * feats, feats), feats), :] = tn(
            joined[:, cols], gp_one[...]
        ).astype(BF16)
        return carry

    lax.fori_loop(0, 2, in_tile, 0)
    trade(3)
    trade(4)

    def late(i, carry):
        rows = pl.ds(pl.multiple_of(i * half, half), half)
        direct[rows, :] = cot[rows, :].astype(F32) + nt(gp_one[rows, :], w_in[:feats, :])
        upd[rows, :] = (
            feat[rows, :].astype(F32) + nn(act_two[rows, :], w_out[...])
        ).astype(BF16)
        return carry

    lax.fori_loop(0, 2, late, 0)

    for q, (at, rows) in enumerate(chunk_list(feats, hid)):
        h = rows // 2
        pairs[q].wait()
        g_half[pl.ds(at // 2, h), :] = (
            grads[pl.ds(pl.multiple_of(at + core * h, h), h), :].astype(F32)
            + g_pair[pl.ds(at // 2, h), :].astype(F32)
        ).astype(BF16)

    for copy in gathers:
        copy.wait()


def middle(part, feat, cot, w_in, w_mid, w_out, ncol):
    n, feats = feat.shape
    hid = w_mid.shape[0]
    shape = jax.ShapeDtypeStruct
    return pl.pallas_call(
        functools.partial(middle_kernel, ncol),
        out_shape=(
            shape((n, feats), BF16),
            shape((n, feats), F32),
            shape((n * ncol, feats), BF16),
            shape(((3 * feats + hid) // 2, hid), BF16),
        ),
        in_specs=in_vmem(6),
        out_specs=tuple(in_vmem(4)),
        scratch_shapes=[
            pltpu.VMEM((3 * feats + hid, hid), BF16),
            pltpu.VMEM(((3 * feats + hid) // 2, hid), BF16),
            pltpu.VMEM((ncol - 1, n, feats), BF16),
            pltpu.VMEM((n, 2 * feats), BF16),
            pltpu.VMEM((n, hid), F32),
            pltpu.VMEM((n, hid), F32),
            pltpu.VMEM((n, hid), BF16),
            pltpu.VMEM((n, hid), BF16),
            pltpu.VMEM((n, hid), BF16),
            pltpu.VMEM((n, hid), BF16),
        ]
        + [pltpu.SemaphoreType.DMA((2, ncol - 1))] * 4
        + [pltpu.SemaphoreType.DMA((5,))] * 2,
        compiler_params=pltpu.CompilerParams(
            collective_id=1, has_side_effects=True, vmem_limit_bytes=VMEM_LIMIT
        ),
        cost_estimate=pl.CostEstimate(
            flops=6 * n * (3 * feats + hid) * hid,
            bytes_accessed=4 * (3 * feats + hid) * hid,
            transcendentals=2 * n * hid,
        ),
    )(part, feat, cot, w_in, w_mid, w_out)


def tail_kernel(
    nrow, ncol, back, direct, g_half,
    nodes, t_out, t_mid, t_in,
    pair_land, pair_sum, chip_land, g_col, g_colsum, g_chip, g_first,
    ps, pr, cs, cr, s1, r1, s2, r2, s3, r3, s4, r4, s5, r5,
):
    r, c = lax.axis_index("row"), lax.axis_index("col")
    chips = nrow // 2
    chip, core = r // 2, lax.rem(r, 2)
    other = 1 - core
    sibling = chip * 2 + other
    n, feats = direct.shape
    hid = g_half.shape[1]
    width = hid // chips
    chunks = chunk_list(feats, hid)
    homes = (
        (g_first, 0), (t_mid, 0), (t_mid, hid // 2), (t_in, 0), (t_in, feats)
    )

    barrier = pltpu.get_barrier_semaphore()
    pl.semaphore_signal(barrier, inc=1, device_id=(sibling, c), device_id_type=MESH)
    for d in range(1, ncol):
        pl.semaphore_signal(barrier, inc=1, device_id=(r, lax.rem(c + d, ncol)), device_id_type=MESH)
    for d in range(1, chips):
        pl.semaphore_signal(
            barrier, inc=1, device_id=(lax.rem(chip + d, chips) * 2 + core, c), device_id_type=MESH
        )
    pl.semaphore_wait(barrier, ncol + chips - 1)

    def send(src, dst, ssem, rsem, device):
        copy = pltpu.make_async_remote_copy(
            src_ref=src, dst_ref=dst, send_sem=ssem, recv_sem=rsem,
            device_id=device, device_id_type=MESH,
        )
        copy.start()
        return copy

    def rows_at(start, size, unit):
        return pl.ds(pl.multiple_of(start, unit), size)

    pair = []
    for d in range(chips):
        z = lax.rem(chip + 1 + d, chips)
        pair.append(
            send(
                back.at[rows_at((z * 2 + other) * n, n, n)],
                pair_land.at[d], ps.at[d], pr.at[d], (sibling, c),
            )
        )

    stage1 = []

    def over_col(q):
        at, rows = chunks[q]
        m = rows // 2 // ncol
        copies = []
        for d in range(1, ncol):
            peer = lax.rem(c + d, ncol)
            copies.append(
                send(
                    g_half.at[rows_at(at // 2 + peer * m, m, 16)],
                    g_col.at[d - 1, pl.ds(at // 2 // ncol, m)],
                    s1.at[q, d - 1], r1.at[q, d - 1], (r, peer),
                )
            )
        stage1.append(copies)

    over_col(0)
    over_col(1)

    across = []

    def across_send(d):
        z = lax.rem(chip + 1 + d, chips)
        across.append(
            send(pair_sum.at[d], chip_land.at[d], cs.at[d], cr.at[d], (z * 2 + core, c))
        )

    late = chips // 4
    for d in range(chips):
        pair[d].wait()
        z = lax.rem(chip + 1 + d, chips)
        pair_sum[d] = (
            back[rows_at((z * 2 + core) * n, n, n), :].astype(F32) + pair_land[d].astype(F32)
        ).astype(BF16)
        if d < chips - 1 - late:
            across_send(d)

    stage2, stage3, stage4, stage5 = [], [], [], []

    def over_chips(q):
        at, rows = chunks[q]
        m = rows // 2 // ncol
        base = at // 2 // ncol
        for copy in stage1[q]:
            copy.wait()
        if q + 2 < len(chunks):
            over_col(q + 2)
        value = g_half[rows_at(at // 2 + c * m, m, 16), :].astype(F32)
        for d in range(1, ncol):
            value = value + g_col[d - 1, pl.ds(base, m), :].astype(F32)
        g_colsum[pl.ds(base, m), :] = value.astype(BF16)
        copies = []
        for d in range(1, chips):
            z = lax.rem(chip + d, chips)
            copies.append(
                send(
                    g_colsum.at[pl.ds(base, m), rows_at(z * width, width, width)],
                    g_chip.at[d - 1, pl.ds(base, m)],
                    s2.at[q, d - 1], r2.at[q, d - 1], (z * 2 + core, c),
                )
            )
        stage2.append(copies)

    def back_over_chips(q):
        at, rows = chunks[q]
        home, first = homes[q]
        h = rows // 2
        m = h // ncol
        base = at // 2 // ncol
        for copy in stage2[q]:
            copy.wait()
        columns = rows_at(chip * width, width, width)
        value = g_colsum[pl.ds(base, m), columns].astype(F32)
        for d in range(1, chips):
            value = value + g_chip[d - 1, pl.ds(base, m), :].astype(F32)
        spot = home.at[rows_at(first + core * h + c * m, m, 16), columns]
        spot[...] = value.astype(BF16)
        copies = []
        for d in range(1, chips):
            z = lax.rem(chip + d, chips)
            copies.append(send(spot, spot, s3.at[q, d - 1], r3.at[q, d - 1], (z * 2 + core, c)))
        stage3.append(copies)

    def back_over_col(q):
        _, rows = chunks[q]
        home, first = homes[q]
        h = rows // 2
        m = h // ncol
        for copy in stage3[q]:
            copy.wait()
        spot = home.at[rows_at(first + core * h + c * m, m, 16)]
        copies = []
        for d in range(1, ncol):
            copies.append(
                send(spot, spot, s4.at[q, d - 1], r4.at[q, d - 1], (r, lax.rem(c + d, ncol)))
            )
        stage4.append(copies)

    def back_to_pair(q):
        _, rows = chunks[q]
        home, first = homes[q]
        h = rows // 2
        for copy in stage4[q]:
            copy.wait()
        spot = home.at[rows_at(first + core * h, h, 16)]
        stage5.append(send(spot, spot, s5.at[q], r5.at[q], (sibling, c)))

    parts = len(chunks)
    for step in range(parts + 2):
        if step < parts:
            over_chips(step)
        if 1 <= step <= parts:
            back_over_chips(step - 1)
        if step >= 2:
            back_over_col(step - 2)
    for d in range(chips - 1 - late, chips - 1):
        across_send(d)
    for q in range(parts - 1):
        back_to_pair(q)
    stage5[0].wait()
    t_out[...] = jnp.transpose(g_first[...].astype(F32)).astype(BF16)
    for copy in across:
        copy.wait()
    value = direct[...] + pair_sum[chips - 1].astype(F32)
    for d in range(chips - 1):
        value = value + chip_land[d].astype(F32)
    nodes[...] = value.astype(BF16)
    back_to_pair(parts - 1)
    for copy in stage5[1:]:
        copy.wait()


def tail(back, direct, g_half, nrow, ncol):
    n, feats = direct.shape
    rows, hid = g_half.shape
    chips = nrow // 2
    parts = len(chunk_list(feats, hid))
    shape = jax.ShapeDtypeStruct
    dma = pltpu.SemaphoreType.DMA
    return pl.pallas_call(
        functools.partial(tail_kernel, nrow, ncol),
        out_shape=(
            shape((n, feats), BF16),
            shape((hid, feats), BF16),
            shape((hid, hid), BF16),
            shape((2 * feats, hid), BF16),
        ),
        in_specs=in_vmem(3),
        out_specs=tuple(in_vmem(4)),
        scratch_shapes=[
            pltpu.VMEM((chips, n, feats), BF16),
            pltpu.VMEM((chips, n, feats), BF16),
            pltpu.VMEM((chips - 1, n, feats), BF16),
            pltpu.VMEM((ncol - 1, rows // ncol, hid), BF16),
            pltpu.VMEM((rows // ncol, hid), BF16),
            pltpu.VMEM((chips - 1, rows // ncol, hid // chips), BF16),
            pltpu.VMEM((feats, hid), BF16),
        ]
        + [dma((chips,))] * 2
        + [dma((chips - 1,))] * 2
        + [dma((parts, ncol - 1))] * 2
        + [dma((parts, chips - 1))] * 4
        + [dma((parts, ncol - 1))] * 2
        + [dma((parts,))] * 2,
        compiler_params=pltpu.CompilerParams(
            collective_id=2, has_side_effects=True, vmem_limit_bytes=VMEM_LIMIT
        ),
    )(back, direct, g_half)


def gather_kernel(nrow, feat, out, own_sem, ss, sr, rs, rr, ls, lr, fs, fr):
    r, c = lax.axis_index("row"), lax.axis_index("col")
    chips = nrow // 2
    chip, core = r // 2, lax.rem(r, 2)
    sibling = chip * 2 + 1 - core
    n = feat.shape[0]
    up, down = chip < chips - 1, chip > 0
    above = lax.rem(chip + 1, chips) * 2 + core
    below = lax.rem(chip + chips - 1, chips) * 2 + core

    def spot(device):
        return out.at[pl.ds(pl.multiple_of(device * n, n), n)]

    def remote(src, dst, ssem, rsem, device):
        return pltpu.make_async_remote_copy(
            src_ref=src, dst_ref=dst, send_sem=ssem, recv_sem=rsem,
            device_id=(device, c), device_id_type=MESH,
        )

    own = pltpu.make_async_copy(feat, spot(r), own_sem)
    own.start()
    barrier = pltpu.get_barrier_semaphore()
    pl.semaphore_signal(barrier, inc=1, device_id=(sibling, c), device_id_type=MESH)

    @pl.when(up)
    def _():
        pl.semaphore_signal(barrier, inc=1, device_id=(above, c), device_id_type=MESH)

    @pl.when(down)
    def _():
        pl.semaphore_signal(barrier, inc=1, device_id=(below, c), device_id_type=MESH)

    pl.semaphore_wait(barrier, 1 + up.astype(jnp.int32) + down.astype(jnp.int32))

    @pl.when(up)
    def _():
        remote(feat, spot(r), rs.at[0], rr.at[0], above).start()

    @pl.when(down)
    def _():
        remote(feat, spot(r), ls.at[0], lr.at[0], below).start()

    near = remote(feat, spot(r), ss, sr, sibling)
    near.start()

    for k in range(1, chips):
        @pl.when(chip >= k)
        def _():
            source = spot(lax.rem(chip - k + chips, chips) * 2 + core)
            remote(source, source, rs.at[k - 1], rr.at[k - 1], below).wait_recv()

            @pl.when(up)
            def _():
                remote(source, source, rs.at[k], rr.at[k], above).start()

            remote(source, source, fs.at[0, k - 1], fr.at[0, k - 1], sibling).start()

        @pl.when(chip + k < chips)
        def _():
            source = spot(lax.rem(chip + k, chips) * 2 + core)
            remote(source, source, ls.at[k - 1], lr.at[k - 1], above).wait_recv()

            @pl.when(down)
            def _():
                remote(source, source, ls.at[k], lr.at[k], below).start()

            remote(source, source, fs.at[1, k - 1], fr.at[1, k - 1], sibling).start()

    own.wait()
    near.wait()
    for k in range(chips):
        @pl.when(up & (chip >= k))
        def _():
            remote(feat, spot(r), rs.at[k], rr.at[k], above).wait_send()

        @pl.when(down & (chip + k < chips))
        def _():
            remote(feat, spot(r), ls.at[k], lr.at[k], below).wait_send()

        if k:
            @pl.when(chip >= k)
            def _():
                source = spot(lax.rem(chip - k + chips, chips) * 2 + core)
                landed = spot(lax.rem(chip - k + chips, chips) * 2 + 1 - core)
                remote(source, landed, fs.at[0, k - 1], fr.at[0, k - 1], sibling).wait()

            @pl.when(chip + k < chips)
            def _():
                source = spot(lax.rem(chip + k, chips) * 2 + core)
                landed = spot(lax.rem(chip + k, chips) * 2 + 1 - core)
                remote(source, landed, fs.at[1, k - 1], fr.at[1, k - 1], sibling).wait()


def gather(feat, nrow):
    n, feats = feat.shape
    chips = nrow // 2
    dma = pltpu.SemaphoreType.DMA
    return pl.pallas_call(
        functools.partial(gather_kernel, nrow),
        out_shape=jax.ShapeDtypeStruct((n * nrow, feats), BF16),
        in_specs=in_vmem(1),
        out_specs=in_vmem(1)[0],
        scratch_shapes=[dma] * 3 + [dma((chips,))] * 4 + [dma((2, chips - 1))] * 2,
        compiler_params=pltpu.CompilerParams(
            collective_id=3, has_side_effects=True, vmem_limit_bytes=VMEM_LIMIT
        ),
    )(feat)


def shards(features, blocks, block_rows, block_cols, block_count, w_in, w_mid, w_out, cotangent):
    nrow, ncol = lax.axis_size("row"), lax.axis_size("col")
    node_dev, feats = features.shape
    hid = w_mid.shape[0]
    cell_blocks = blocks[0, 0]
    rows_here = block_rows[0, 0]
    cols_here = block_cols[0, 0]
    count = block_count[0]
    column_feats = gather(features, nrow)
    part = cell_term(
        cell_blocks, cols_here, rows_here, count, column_feats, node_dev * ncol, False
    )
    updated, direct, row_grads, grads = middle(
        part, features, cotangent, w_in, w_mid, w_out, ncol
    )
    back = cell_term(
        cell_blocks, rows_here, cols_here, count, row_grads, node_dev * nrow, True
    )
    grad_nodes, sum_out, sum_mid, sum_in = tail(back, direct, grads, nrow, ncol)
    ratio = 1.0 / math.sqrt(node_dev * nrow * ncol)
    return (
        updated,
        grad_nodes,
        sum_in.astype(F32) * ratio,
        sum_mid.astype(F32) * ratio,
        sum_out.astype(F32) * ratio,
    )


def solution(mesh):
    placed = (
        P(("row", "col"), None),
        P("row", "col", None, None, None),
        P("row", "col", None),
        P("row", "col", None),
        P("row", "col"),
        P(),
        P(),
        P(),
        P(("row", "col"), None),
    )
    return jax.shard_map(
        shards,
        mesh=mesh,
        in_specs=placed,
        out_specs=(P(("row", "col"), None), P(("row", "col"), None), P(), P(), P()),
        check_vma=False,
    )
```
